32 devices in a mesh: row: 4 (over y, core), col: 8 (over z, x).
Axes of the slice: x: 2, y: 2, z: 4, core: 2. Of those that a mesh axis runs over, the one named last changes fastest.
Arguments:
- hidden: bfloat16 [8192, 4608], P('col', 'row'), may hold values from -6 to 6
- w_query: bfloat16 [4608, 4096], P('col', 'row'), may hold values from -0.09375 to 0.09375
- w_key: bfloat16 [4608, 2048], P('col', 'row'), may hold values from -0.09375 to 0.09375
- w_value: bfloat16 [4608, 2048], P('col', 'row'), may hold values from -0.09375 to 0.09375
- adapter_down: bfloat16 [8, 4608, 32], P('col', 'row'), may hold values from -0.09375 to 0.09375
- adapter_up_query: bfloat16 [8, 16, 4096], P('col', None, 'row'), may hold values from -1.5 to 1.5
- adapter_up_value: bfloat16 [8, 16, 2048], P('col', None, 'row'), may hold values from -1.5 to 1.5
- lengths: int32 [8, 10], P('col'), may hold values from 1 to 192, 1024 in all within a row
- request_adapter: int32 [8, 10], P('col'), may hold values from 0 to 7
- adapter_slot: int32 [8], replicated, may hold values from 0 to 7, each once
- page_table: int32 [8, 18], P('col'), may hold values from 0 to 17, each once within a row
Outputs:
- query: bfloat16 [8192, 4096], P('col', 'row')
- key_cache: bfloat16 [144, 128, 2048], P('col', None, 'row')
- value_cache: bfloat16 [144, 128, 2048], P('col', None, 'row')
The draws below stay inside these ranges and needn't reach their ends.
Inputs may be any that keep to these rules, and one draw needn't show every extreme that they name: Each row of lengths sums to 1024, and its longest request has exactly 192 tokens. `adapter_slot`: a permutation of the slots. `page_table`: each row is a permutation of the 18 local slots.
All inputs are finite; a program needn't handle non-finite values.
Results may differ from the reference program's by a relative error of at most 0.0039.
Values may be sent and summed in bfloat16 or wider, within the bound.
A program may use at most 128 MiB of HBM per device.

```python
import math
import jax
import jax.numpy as jnp
import numpy as np

D = 4608
HEAD = 128
RANK = 16
PAGE = 128
MOST = 192
TOK_DEV = 1024
REQ_DEV = 10
PAGES_DEV = 18
QW = 4096
KW = 2048
ADAPTERS = 8
TOKENS = 8192
CACHE_PAGES = 144
N_COL = 8


def plant(entries, rng, least, top_value):
    longest = entries.shape.index(max(entries.shape))
    spots = []
    for shift in (0, 1):
        where = [jax.random.randint(jax.random.fold_in(rng, axis), (), 0, length) for axis, length in enumerate(entries.shape)]
        where[longest] = (where[longest] + shift) % entries.shape[longest]
        spots.append(tuple(where))
    return entries.at[spots[0]].set(least).at[spots[1]].set(top_value)


def block_scale(rng, extent, shards, smallest, top_value):
    gain = 1.0
    for dim, shards_of in shards:
        draws = jax.random.uniform(jax.random.fold_in(jax.random.fold_in(rng, 6), dim), (shards_of,), jnp.float32, smallest / len(shards), top_value / len(shards))
        gain = gain * jnp.repeat(jnp.exp(draws), extent[dim] // shards_of).reshape((-1,) + (1,) * (len(extent) - 1 - dim))
    return gain


def rank_table(number_of, lean):
    weights = [(1 << 20) // math.isqrt(rank ** lean) + 1 for rank in range(1, number_of + 1)]
    scale = 1 + sum(weights) // (1 << 30)
    return np.cumsum(np.array([max(1, weight // scale) for weight in weights]))


def ranked(own_key, extent, amount, lean):
    listing = rank_table(amount, lean)
    ticket = jax.random.randint(jax.random.fold_in(own_key, 1), extent, 0, int(listing[amount - 1]))
    grade = jnp.searchsorted(jnp.asarray(listing, jnp.int32), ticket, side="right")
    return jax.random.permutation(jax.random.fold_in(own_key, 2), amount)[grade].astype(jnp.int32)


def length_profile(amount, total, limit, lean):
    portions = [(1 << 20) // math.isqrt(grade ** lean) + 1 for grade in range(2, amount + 1)]
    spare, given = total - limit - (amount - 1), [1] * (amount - 1)
    while spare > 0:
        candidates = [i for i in range(amount - 1) if given[i] < limit]
        mass, budget = sum([portions[i] for i in candidates]), spare
        for i in candidates:
            addition = min(limit - given[i], max(1, budget * portions[i] // mass), spare)
            given[i] = given[i] + addition
            spare = spare - addition
    return np.array([limit] + given)


def ragged(key, number_of, total, bound, skew):
    if number_of == 2:
        one = jax.random.randint(key, (), max(1, total - bound), min(bound, total - 1) + 1)
        return jnp.stack([one, total - one])
    tallies = jnp.asarray(length_profile(number_of, total, bound, skew), jnp.int32)
    couples = (number_of - 1) // 2
    source_of, sink = tallies[1:1 + 2 * couples:2], tallies[2:2 + 2 * couples:2]
    slack = jnp.minimum(source_of - 1, bound - sink)
    shifted = jax.random.randint(jax.random.fold_in(key, 1), (couples,), 0, 1 << 20) % (slack + 1)
    tallies = tallies.at[1:1 + 2 * couples:2].set(source_of - shifted).at[2:2 + 2 * couples:2].set(sink + shifted)
    return tallies[jax.random.permutation(jax.random.fold_in(key, 2), number_of)]


def bell_draw(own_key, extent, spread, limit, cuts=(), held_as=jnp.bfloat16):
    factor_of = block_scale(own_key, extent, cuts, -0.22, 0.18) if cuts else 1.0
    entries = jax.random.normal(own_key, extent, jnp.float32) * spread * factor_of
    return jnp.minimum(jnp.maximum(entries, -limit), limit).astype(held_as)


def setup_inputs(seed: int = 0) -> dict:
    streams_of = jax.random.split(jax.random.key(seed), 12)
    hidden = bell_draw(streams_of[0], (TOKENS, D), 1.0, 6.0, ((0, 8), (1, 4)))
    w_query = bell_draw(streams_of[1], (D, QW), D ** -0.5, 0.09375, ((0, 8), (1, 4)))
    w_key = bell_draw(streams_of[2], (D, KW), D ** -0.5, 0.09375, ((0, 8), (1, 4)))
    w_value = bell_draw(streams_of[3], (D, KW), D ** -0.5, 0.09375, ((0, 8), (1, 4)))
    adapter_down = bell_draw(streams_of[4], (ADAPTERS, D, 2 * RANK), D ** -0.5, 0.09375, ((0, 8), (1, 4)))
    adapter_up_query = bell_draw(streams_of[5], (ADAPTERS, RANK, QW), RANK ** -0.5, 1.5, ((0, 8), (2, 4)))
    adapter_up_value = bell_draw(streams_of[6], (ADAPTERS, RANK, KW), RANK ** -0.5, 1.5, ((0, 8), (2, 4)))
    lengths = jax.vmap(lambda own: ragged(own, REQ_DEV, TOK_DEV, MOST, 2))(jax.random.split(streams_of[7], N_COL)).reshape((N_COL, REQ_DEV)).astype(jnp.int32)
    request_adapter = plant(ranked(streams_of[8], (N_COL, REQ_DEV), ADAPTERS, 2), jax.random.fold_in(streams_of[8], 3), 0, ADAPTERS - 1).astype(jnp.int32)
    adapter_slot = jax.random.permutation(streams_of[9], ADAPTERS).astype(jnp.int32)
    page_table = jax.vmap(lambda own: jax.random.permutation(own, PAGES_DEV))(jax.random.split(streams_of[10], N_COL)).reshape((N_COL, PAGES_DEV)).astype(jnp.int32)
    return dict(hidden=hidden, w_query=w_query, w_key=w_key, w_value=w_value, adapter_down=adapter_down, adapter_up_query=adapter_up_query, adapter_up_value=adapter_up_value, lengths=lengths, request_adapter=request_adapter, adapter_slot=adapter_slot, page_table=page_table)


def rotate(values, position):
    half_width = HEAD // 2
    frequency = jnp.exp(jnp.arange(half_width, dtype=jnp.float32) * (-2.0 * math.log(10000.0) / HEAD))
    angles = position.astype(jnp.float32)[:, None] * frequency[None, :]
    cosine = jnp.cos(angles)[:, None, :]
    sine_value = jnp.sin(angles)[:, None, :]
    shaped = values.reshape(values.shape[0], -1, HEAD)
    leading = shaped[:, :, :half_width]
    second = shaped[:, :, half_width:]
    rotated = jnp.concatenate([leading * cosine - second * sine_value, second * cosine + leading * sine_value], axis=2)
    return rotated.reshape(values.shape)


def layout(lengths, page_row):
    token_index = jnp.arange(TOK_DEV, dtype=jnp.int32)
    starts = (jnp.cumsum(lengths) - lengths).astype(jnp.int32)
    request_of = (jnp.sum((token_index[:, None] >= starts[None, :]).astype(jnp.int32), axis=1) - 1).astype(jnp.int32)
    position = (token_index - jnp.take(starts, request_of)).astype(jnp.int32)
    pages_each = ((lengths + PAGE - 1) // PAGE).astype(jnp.int32)
    page_start = (jnp.cumsum(pages_each) - pages_each).astype(jnp.int32)
    page_index = (jnp.take(page_start, request_of) + position // PAGE).astype(jnp.int32)
    target = (jnp.take(page_row, page_index) * PAGE + position % PAGE).astype(jnp.int32)
    return starts, request_of, position, target


def expand_up(lowrank, chosen, up_query, up_value):
    adapter_count = up_query.shape[0]
    rank_width = up_query.shape[1]
    onehot = (chosen[:, None] == jnp.arange(adapter_count, dtype=jnp.int32)[None, :]).astype(lowrank.dtype)
    spread_query = (onehot[:, :, None] * lowrank[:, None, :rank_width]).reshape(-1, adapter_count * rank_width)
    spread_value = (onehot[:, :, None] * lowrank[:, None, rank_width:]).reshape(-1, adapter_count * rank_width)
    delta_query = jnp.dot(spread_query, up_query.reshape(adapter_count * rank_width, -1), preferred_element_type=jnp.float32)
    delta_value = jnp.dot(spread_value, up_value.reshape(adapter_count * rank_width, -1), preferred_element_type=jnp.float32)
    return delta_query, delta_value


def reference(hidden, w_query, w_key, w_value, adapter_down, adapter_up_query, adapter_up_value, lengths, request_adapter, adapter_slot, page_table):
    starts, request_of, position, target = jax.vmap(layout)(lengths, page_table)
    offsets = (jnp.arange(N_COL, dtype=jnp.int32) * (PAGES_DEV * PAGE))[:, None]
    target = (target + offsets).reshape(-1)
    position = position.reshape(-1)
    chosen = jnp.take(adapter_slot, jnp.take_along_axis(request_adapter, request_of, axis=1)).reshape(-1)
    base_query = jnp.dot(hidden, w_query, preferred_element_type=jnp.float32)
    base_key = jnp.dot(hidden, w_key, preferred_element_type=jnp.float32)
    base_value = jnp.dot(hidden, w_value, preferred_element_type=jnp.float32)
    stacked_down = jnp.transpose(adapter_down, (1, 0, 2)).reshape(D, ADAPTERS * 2 * RANK)
    lowrank_all = jnp.dot(hidden, stacked_down, preferred_element_type=jnp.float32).reshape(-1, ADAPTERS, 2 * RANK)
    lowrank = jnp.take_along_axis(lowrank_all, chosen[:, None, None], axis=1)[:, 0].astype(jnp.bfloat16)
    delta_query, delta_value = expand_up(lowrank, chosen, adapter_up_query, adapter_up_value)
    query = rotate(base_query + delta_query, position).astype(jnp.bfloat16)
    key_rotated = rotate(base_key, position).astype(jnp.bfloat16)
    value_rows = (base_value + delta_value).astype(jnp.bfloat16)
    key_cache = jnp.zeros((CACHE_PAGES * PAGE, KW), jnp.bfloat16).at[target].set(key_rotated).reshape(CACHE_PAGES, PAGE, KW)
    value_cache = jnp.zeros((CACHE_PAGES * PAGE, KW), jnp.bfloat16).at[target].set(value_rows).reshape(CACHE_PAGES, PAGE, KW)
    return (query, key_cache, value_cache)
```

```python
import functools
import math

import jax
import jax.numpy as jnp
from jax import lax
from jax.experimental import pallas as pl
from jax.experimental.pallas import tpu as pltpu
from jax.sharding import PartitionSpec as P

HEAD = 128
PAGE = 128
TOK = 1024
CHUNKS = 8
AHEAD = 3
TILE = 256
MESH = pl.DeviceIdType.MESH
BF16 = jnp.bfloat16
F32 = jnp.float32


def project(nc, nr, h2, w, raw, dn_in, up_in, pos, slot, freq, q_out, kv_out,
            wbuf, hid, acc, sendb, precv, dn, up, lr, sq, sv, cosb, sinb,
            local, wsend, wrecv, hsend, hrecv, csend, xsend, xrecv,
            psend, pget, dsend, drecv, usend, urecv, lsend, lrecv):
    nb = nc // 2
    per = nb // nr
    kb, cw = wbuf.shape[2], wbuf.shape[3]
    rank = up_in.shape[0]
    kw = kv_out.shape[1] // 2
    c = lax.axis_index("col")
    r = lax.axis_index("row")
    p = c // 2
    x = c % 2
    other = 1 - x
    mate = c + 1 - 2 * x
    twin = r + 1 - 2 * (r % 2)

    def remote(src, dst, ssem, rsem, **where):
        return pltpu.make_async_remote_copy(
            src_ref=src, dst_ref=dst, send_sem=ssem, recv_sem=rsem,
            device_id=where, device_id_type=MESH)

    loads = [
        pltpu.make_async_copy(w, wbuf.at[p], local.at[0]),
        pltpu.make_async_copy(h2.at[x], hid.at[r, x], local.at[1]),
        pltpu.make_async_copy(dn_in, dn.at[c], local.at[2]),
        pltpu.make_async_copy(up_in, up.at[c], local.at[3]),
    ]
    for one in loads:
        one.start()

    barrier = pltpu.get_barrier_semaphore()

    @pl.loop(1, nc)
    def _(m):
        pl.semaphore_signal(barrier, inc=1, device_id={"col": (c + m) % nc}, device_id_type=MESH)

    @pl.loop(1, nr)
    def _(m):
        pl.semaphore_signal(barrier, inc=1, device_id={"row": (r + m) % nr}, device_id_type=MESH)

    pl.semaphore_wait(barrier, nc + nr - 2)
    for one in loads:
        one.wait()

    def weight(b, j, side):
        to = jnp.clip(c + 2 if side else c - 2, 0, nc - 1)
        return remote(wbuf.at[b, j], wbuf.at[b, j], wsend.at[side, b, j], wrecv.at[b, j], col=to)

    def send_own(j):
        @pl.when(p + 1 < nb)
        def _():
            weight(p, j, 1).start()

        @pl.when(p > 0)
        def _():
            weight(p, j, 0).start()

    def service(j):
        @pl.loop(1, nb)
        def _(d):
            @pl.when(p - d >= 0)
            def _():
                weight(p - d, j, 1).wait_recv()

                @pl.when(p + 1 < nb)
                def _():
                    weight(p - d, j, 1).start()

            @pl.when(p + d < nb)
            def _():
                weight(p + d, j, 0).wait_recv()

                @pl.when(p > 0)
                def _():
                    weight(p + d, j, 0).start()

        if j + AHEAD < CHUNKS:
            send_own(j + AHEAD)

    def to_mate():
        return remote(h2.at[other], hid.at[r, x], xsend, xrecv, col=mate)

    def from_mate():
        return remote(h2.at[other], hid.at[r, other], xsend, xrecv, col=mate)

    def to_peer(t, m):
        return remote(hid.at[r, t], hid.at[r, t], hsend.at[t, m], hrecv.at[r, t], row=(r + 2 * m) % nr)

    def to_twin(o, t):
        return remote(hid.at[o, t], hid.at[o, t], csend.at[o, t], hrecv.at[o, t], row=twin)

    def arrived(o, t):
        remote(hid.at[o, t], hid.at[o, t], csend.at[o, t], hrecv.at[o, t], row=twin).wait_recv()

    def spread_hidden(t):
        for m in range(1, nr // 2):
            to_peer(t, m).start()
        to_twin(r, t).start()

    def pass_hidden(t):
        for m in range(1, nr // 2):
            o = (r + 2 * m) % nr
            arrived(o, t)
            to_twin(o, t).start()

    def settle_hidden(t):
        for m in range(nr // 2):
            arrived((twin + 2 * m) % nr, t)

    def down_copy(owner, m):
        return remote(dn.at[owner], dn.at[owner], dsend.at[m], drecv.at[owner], col=(c + m) % nc)

    def up_copy(owner, m):
        return remote(up.at[owner], up.at[owner], usend.at[m], urecv.at[owner], col=(c + m) % nc)

    def low_copy(owner, m):
        return remote(lr.at[owner], lr.at[owner], lsend.at[m], lrecv.at[owner], row=(r + m) % nr)

    def lowrank_start():
        @pl.loop(1, nc)
        def _(m):
            down_copy((c + m) % nc, m).wait_recv()

        everything = lax.dot_general(
            dn[...].reshape(nc * 2 * rank, raw.shape[1]), raw[...],
            (((1,), (1,)), ((), ())), preferred_element_type=F32)
        which = slot[...]
        mine = jnp.zeros((2 * rank, TOK), F32)
        for a in range(nc):
            mine = mine + jnp.where(which == a, everything[a * 2 * rank:(a + 1) * 2 * rank], 0.0)
        lr[r] = mine

        @pl.loop(1, nr)
        def _(m):
            low_copy(r, m).start()

    def lowrank_end():
        @pl.loop(1, nr)
        def _(m):
            low_copy((r + m) % nr, m).wait_recv()

        @pl.loop(1, nc)
        def _(m):
            up_copy((c + m) % nc, m).wait_recv()

        total = lr[0]
        for o in range(1, nr):
            total = total + lr[o]
        which = slot[...]
        for ref, part in ((sq, total[:rank]), (sv, total[rank:])):
            tall = jnp.concatenate([jnp.where(which == a, part, 0.0) for a in range(nc)], axis=0)
            ref[...] = tall.T.astype(BF16)

    def tables():
        @pl.loop(0, TOK // TILE)
        def _(i):
            rows = pl.ds(pl.multiple_of(i * TILE, TILE), TILE)
            angle = pos[rows, :] * freq[...]
            sign = jnp.where(lax.broadcasted_iota(jnp.int32, (TILE, HEAD), 1) < HEAD // 2, -1.0, 1.0)
            cosb[rows, :] = jnp.cos(angle)
            sinb[rows, :] = jnp.sin(angle) * sign

    def product(j, half, rows):
        total = None
        for o in range(nr):
            factor = wbuf[o * per:(o + 1) * per, j].reshape(per * kb, cw)
            term = jnp.dot(hid[o, half, rows, :], factor, preferred_element_type=F32)
            total = term if total is None else total + term
        return total

    def part_copy(j):
        return remote(sendb.at[j], precv.at[j], psend.at[j], pget.at[j], col=mate)

    def compute(j):
        @pl.loop(0, TOK // TILE)
        def _(i):
            rows = pl.ds(pl.multiple_of(i * TILE, TILE), TILE)
            sendb[j, rows, :] = product(j, other, rows).astype(BF16)

        part_copy(j).start()

        @pl.loop(0, TOK // TILE)
        def _(i):
            rows = pl.ds(pl.multiple_of(i * TILE, TILE), TILE)
            acc[j, rows, :] = product(j, x, rows)

    def combine(j):
        part_copy(j).wait_recv()

        @pl.loop(0, TOK // TILE)
        def _(i):
            rows = pl.ds(pl.multiple_of(i * TILE, TILE), TILE)
            v = acc[j, rows, :] + precv[j, rows, :].astype(F32)
            if j >= 2:
                at = (j - 2) * cw
                factor = up[:, :, at:at + cw].reshape(nc * rank, cw)
                lowered = sq if j < 6 else sv
                v = v + jnp.dot(lowered[rows, :], factor, preferred_element_type=F32)
            if j < 6:
                heads = []
                for k in range(cw // HEAD):
                    one = v[:, k * HEAD:(k + 1) * HEAD]
                    heads.append(one * cosb[rows, :] + pltpu.roll(one, HEAD // 2, 1) * sinb[rows, :])
                v = heads[0] if len(heads) == 1 else jnp.concatenate(heads, axis=1)
            v = v.astype(BF16)
            if j < 2:
                kv_out[rows, j * cw:(j + 1) * cw] = v
            elif j < 6:
                q_out[rows, (j - 2) * cw:(j - 1) * cw] = v
            else:
                kv_out[rows, kw + (j - 6) * cw:kw + (j - 5) * cw] = v

    to_mate().start()
    spread_hidden(x)
    send_own(0)

    @pl.loop(1, nc)
    def _(m):
        down_copy(c, m).start()
        up_copy(c, m).start()

    for j in range(1, AHEAD):
        send_own(j)
    tables()
    service(0)
    from_mate().wait_recv()
    spread_hidden(other)
    pass_hidden(x)
    service(1)
    lowrank_start()
    service(2)
    pass_hidden(other)
    settle_hidden(x)
    settle_hidden(other)
    compute(0)
    service(3)
    compute(1)
    compute(2)
    lowrank_end()
    service(4)
    combine(0)
    compute(3)
    compute(4)
    combine(1)
    for j in range(5, CHUNKS):
        service(j)
        compute(j)
        combine(j - 3)
    for j in range(CHUNKS - 3, CHUNKS):
        combine(j)

    @pl.loop(0, CHUNKS)
    def _(j):
        @pl.loop(0, nb)
        def _(b):
            @pl.when((b <= p) & (p + 1 < nb))
            def _():
                weight(b, j, 1).wait_send()

            @pl.when((b >= p) & (p > 0))
            def _():
                weight(b, j, 0).wait_send()

        part_copy(j).wait_send()

    to_mate().wait_send()
    for t in range(2):
        for m in range(1, nr // 2):
            to_peer(t, m).wait_send()
        for m in range(nr // 2):
            to_twin((r + 2 * m) % nr, t).wait_send()

    @pl.loop(1, nc)
    def _(m):
        down_copy(c, m).wait_send()
        up_copy(c, m).wait_send()

    @pl.loop(1, nr)
    def _(m):
        low_copy(r, m).wait_send()


def paging(table, first, count, kv, key, value):
    n = pl.program_id(0)
    window = PAGE + 16
    kw = key.shape[2]
    base = pl.multiple_of(jnp.minimum(first[n] // 16 * 16, TOK - window), 16)
    row = lax.broadcasted_iota(jnp.int32, (PAGE, window), 0)
    column = lax.broadcasted_iota(jnp.int32, (PAGE, window), 1)
    pick = ((column == row + (first[n] - base)) & (row < count[n])).astype(F32).astype(BF16)
    rows = jnp.dot(pick, kv[pl.ds(base, window), :], preferred_element_type=F32).astype(BF16)
    key[0] = rows[:, :kw]
    value[0] = rows[:, kw:]


def shards(nc, nr, hidden, w_query, w_key, w_value, adapter_down, adapter_up_query,
           adapter_up_value, lengths, request_adapter, adapter_slot, page_table):
    kb = w_query.shape[0]
    qw, kw = w_query.shape[1], w_key.shape[1]
    width = qw + 2 * kw
    cw = width // CHUNKS
    hw = hidden.shape[1]
    rank = adapter_up_query.shape[1]
    pages = page_table.shape[1]
    nb = nc // 2

    lengths, page_row = lengths[0], page_table[0]
    starts = jnp.cumsum(lengths) - lengths
    token = jnp.arange(TOK, dtype=jnp.int32)
    after = token[:, None] >= starts[None, :]
    within = after & (token[:, None] < (starts + lengths)[None, :])
    position = token - jnp.max(jnp.where(after, starts[None, :], 0), axis=1)
    adapters = jnp.arange(nc, dtype=jnp.int32)
    chosen_request = jnp.sum(
        jnp.where(request_adapter[0][:, None] == adapters[None, :], adapter_slot[None, :], 0), axis=1)
    chosen = jnp.sum(jnp.where(within, chosen_request[None, :], 0), axis=1)
    frequency = jnp.exp(jnp.arange(HEAD // 2, dtype=F32) * (-2.0 * math.log(10000.0) / HEAD))
    frequency = jnp.concatenate([frequency, frequency])[None, :]

    pages_each = (lengths + PAGE - 1) // PAGE
    page_start = jnp.cumsum(pages_each) - pages_each
    number = jnp.arange(pages, dtype=jnp.int32)
    started = number[:, None] >= page_start[None, :]
    owner = jnp.sum(started.astype(jnp.int32), axis=1) - 1
    mine = owner[:, None] == jnp.arange(lengths.shape[0], dtype=jnp.int32)[None, :]
    offset = (number - jnp.sum(jnp.where(mine, page_start[None, :], 0), axis=1)) * PAGE
    first = jnp.minimum(jnp.sum(jnp.where(mine, starts[None, :], 0), axis=1) + offset, TOK - 1)
    count = jnp.clip(jnp.sum(jnp.where(mine, lengths[None, :], 0), axis=1) - offset, 0, PAGE)

    w = jnp.concatenate([w_key, w_query, w_value], axis=1)
    w = w.reshape(kb, CHUNKS, cw).transpose(1, 0, 2)
    h2 = hidden.reshape(TOK, hw // (2 * kb), 2, kb).transpose(2, 0, 1, 3).reshape(2, TOK, hw // 2)
    down = adapter_down[0].T
    up = jnp.concatenate([adapter_up_query[0], adapter_up_value[0]], axis=1)

    hbm = pl.BlockSpec(memory_space=pl.ANY)
    vmem = pl.BlockSpec(memory_space=pltpu.VMEM)
    dma = pltpu.SemaphoreType.DMA
    query, kv = pl.pallas_call(
        functools.partial(project, nc, nr),
        out_shape=(jax.ShapeDtypeStruct((TOK, qw), BF16), jax.ShapeDtypeStruct((TOK, 2 * kw), BF16)),
        in_specs=[hbm, hbm, vmem, hbm, hbm, vmem, vmem, vmem],
        out_specs=(vmem, vmem),
        scratch_shapes=[
            pltpu.VMEM((nb, CHUNKS, kb, cw), BF16),
            pltpu.VMEM((nr, 2, TOK, hw // 2), BF16),
            pltpu.VMEM((CHUNKS, TOK, cw), F32),
            pltpu.VMEM((CHUNKS, TOK, cw), BF16),
            pltpu.VMEM((CHUNKS, TOK, cw), BF16),
            pltpu.VMEM((nc, 2 * rank, hw), BF16),
            pltpu.VMEM((nc, rank, qw + kw), BF16),
            pltpu.VMEM((nr, 2 * rank, TOK), F32),
            pltpu.VMEM((TOK, nc * rank), BF16),
            pltpu.VMEM((TOK, nc * rank), BF16),
            pltpu.VMEM((TOK, HEAD), F32),
            pltpu.VMEM((TOK, HEAD), F32),
            dma((4,)),
            dma((2, nb, CHUNKS)),
            dma((nb, CHUNKS)),
            dma((2, nr)),
            dma((nr, 2)),
            dma((nr, 2)),
            dma,
            dma,
            dma((CHUNKS,)),
            dma((CHUNKS,)),
            dma((nc,)),
            dma((nc,)),
            dma((nc,)),
            dma((nc,)),
            dma((nr,)),
            dma((nr,)),
        ],
        compiler_params=pltpu.CompilerParams(
            collective_id=0, has_side_effects=True, vmem_limit_bytes=60 * 1024 * 1024),
        name="project",
    )(h2, w, hidden, down, up, position.astype(F32)[:, None], chosen[None, :], frequency)

    key_cache, value_cache = pl.pallas_call(
        paging,
        out_shape=(jax.ShapeDtypeStruct((pages, PAGE, kw), BF16),) * 2,
        grid_spec=pltpu.PrefetchScalarGridSpec(
            num_scalar_prefetch=3,
            grid=(pages,),
            in_specs=[pl.BlockSpec((TOK, 2 * kw), lambda n, table, first, count: (0, 0))],
            out_specs=[pl.BlockSpec((1, PAGE, kw), lambda n, table, first, count: (table[n], 0, 0))] * 2,
        ),
        compiler_params=pltpu.CompilerParams(vmem_limit_bytes=32 * 1024 * 1024),
        name="paging",
    )(page_row, first, count, kv)
    return (query, key_cache, value_cache)


def solution(mesh):
    return jax.shard_map(
        functools.partial(shards, mesh.shape["col"], mesh.shape["row"]),
        mesh=mesh,
        in_specs=(
            P("col", "row"),
            P("col", "row"),
            P("col", "row"),
            P("col", "row"),
            P("col", "row", None),
            P("col", None, "row"),
            P("col", None, "row"),
            P("col", None),
            P("col", None),
            P(),
            P("col", None),
        ),
        out_specs=(P("col", "row"), P("col", None, "row"), P("col", None, "row")),
        check_vma=False,
    )
```

```python
import functools
import math

import jax
import jax.numpy as jnp
import numpy as np
from jax import lax
from jax.experimental import pallas as pl
from jax.experimental.pallas import tpu as pltpu
from jax.sharding import PartitionSpec as P

HEAD = 128
PAGE = 128
TOK = 1024
CHUNKS = 8
AHEAD = 3
TILE = 256
HALF = 512
MESH = pl.DeviceIdType.MESH
BF16 = jnp.bfloat16
F32 = jnp.float32


def project(nc, nr, raw, w_query, w_key, w_value, dn_in, upq_in, upv_in, freq,
            lengths, request_adapter, adapter_slot, q_out, kv_out,
            wbuf, h2, hid, acc, sendb, precv, dn, up, lr, sq, sv, cosb, sinb,
            wload, local, wsend, wrecv, hsend, hrecv, csend, xsend, xrecv,
            psend, pget, dsend, dmate, drecv, usend, umate, urecv, lsend, lrecv):
    nb = nc // 2
    per = nb // nr
    kb, cw = wbuf.shape[2], wbuf.shape[3]
    rank = upq_in.shape[1]
    qw = upq_in.shape[2]
    kw = kv_out.shape[1] // 2
    c = lax.axis_index("col")
    r = lax.axis_index("row")
    p = c // 2
    x = c % 2
    other = 1 - x
    mate = c + 1 - 2 * x
    twin = r + 1 - 2 * (r % 2)

    def remote(src, dst, ssem, rsem, **where):
        return pltpu.make_async_remote_copy(
            src_ref=src, dst_ref=dst, send_sem=ssem, recv_sem=rsem,
            device_id=where, device_id_type=MESH)

    loads = [
        pltpu.make_async_copy(dn_in, dn.at[c], local.at[0]),
        pltpu.make_async_copy(upq_in.at[0], up.at[c, :, :qw], local.at[1]),
        pltpu.make_async_copy(upv_in.at[0], up.at[c, :, qw:], local.at[2]),
    ]
    for j in range(CHUNKS):
        if j < 2:
            src, at = w_key, j * cw
        elif j < 6:
            src, at = w_query, (j - 2) * cw
        else:
            src, at = w_value, (j - 6) * cw
        loads.append(pltpu.make_async_copy(src.at[:, at:at + cw], wbuf.at[p, j], wload.at[j]))
    for one in loads:
        one.start()

    @pl.loop(0, TOK // TILE)
    def _(i):
        rows = pl.ds(pl.multiple_of(i * TILE, TILE), TILE)
        for s in range(2):
            parts = [raw[rows, (2 * g + s) * kb:(2 * g + s + 1) * kb] for g in range(per)]
            h2[s, rows, :] = parts[0] if per == 1 else jnp.concatenate(parts, axis=1)
        hid[r, x, rows, :] = h2[x, rows, :]

    barrier = pltpu.get_barrier_semaphore()

    @pl.loop(1, nc)
    def _(m):
        pl.semaphore_signal(barrier, inc=1, device_id={"col": (c + m) % nc}, device_id_type=MESH)

    @pl.loop(1, nr)
    def _(m):
        pl.semaphore_signal(barrier, inc=1, device_id={"row": (r + m) % nr}, device_id_type=MESH)

    pl.semaphore_wait(barrier, nc + nr - 2)
    for one in loads:
        one.wait()

    def weight(b, j, side):
        to = jnp.clip(c + 2 if side else c - 2, 0, nc - 1)
        return remote(wbuf.at[b, j], wbuf.at[b, j], wsend.at[side, b, j], wrecv.at[b, j], col=to)

    def send_own(j):
        @pl.when(p + 1 < nb)
        def _():
            weight(p, j, 1).start()

        @pl.when(p > 0)
        def _():
            weight(p, j, 0).start()

    def service(j):
        @pl.loop(1, nb)
        def _(d):
            @pl.when(p - d >= 0)
            def _():
                weight(p - d, j, 1).wait_recv()

                @pl.when(p + 1 < nb)
                def _():
                    weight(p - d, j, 1).start()

            @pl.when(p + d < nb)
            def _():
                weight(p + d, j, 0).wait_recv()

                @pl.when(p > 0)
                def _():
                    weight(p + d, j, 0).start()

        if j + AHEAD < CHUNKS:
            send_own(j + AHEAD)

    def to_mate():
        return remote(h2.at[other], hid.at[r, x], xsend, xrecv, col=mate)

    def from_mate():
        return remote(h2.at[other], hid.at[r, other], xsend, xrecv, col=mate)

    def to_peer(t, m):
        return remote(hid.at[r, t], hid.at[r, t], hsend.at[t, m], hrecv.at[r, t], row=(r + 2 * m) % nr)

    def to_twin(o, t):
        return remote(hid.at[o, t], hid.at[o, t], csend.at[o, t], hrecv.at[o, t], row=twin)

    def arrived(o, t):
        remote(hid.at[o, t], hid.at[o, t], csend.at[o, t], hrecv.at[o, t], row=twin).wait_recv()

    def spread_hidden(t):
        for m in range(1, nr // 2):
            to_peer(t, m).start()
        to_twin(r, t).start()

    def pass_hidden(t):
        for m in range(1, nr // 2):
            o = (r + 2 * m) % nr
            arrived(o, t)
            to_twin(o, t).start()

    def settle_hidden(t):
        for m in range(nr // 2):
            arrived((twin + 2 * m) % nr, t)

    def factors(b, side):
        owner = 2 * b + x
        to = jnp.clip(c + 2 if side else c - 2, 0, nc - 1)
        return (remote(dn.at[owner], dn.at[owner], dsend.at[side, b], drecv.at[owner], col=to),
                remote(up.at[owner], up.at[owner], usend.at[side, b], urecv.at[owner], col=to))

    def factors_mate(b, parity):
        owner = 2 * b + parity
        return (remote(dn.at[owner], dn.at[owner], dmate.at[b], drecv.at[owner], col=mate),
                remote(up.at[owner], up.at[owner], umate.at[b], urecv.at[owner], col=mate))

    def start(pair):
        for one in pair:
            one.start()

    def send_factors():
        @pl.when(p + 1 < nb)
        def _():
            start(factors(p, 1))

        @pl.when(p > 0)
        def _():
            start(factors(p, 0))

        start(factors_mate(p, x))

    def service_factors():
        @pl.loop(1, nb)
        def _(d):
            @pl.when(p - d >= 0)
            def _():
                for one in factors(p - d, 1):
                    one.wait_recv()

                @pl.when(p + 1 < nb)
                def _():
                    start(factors(p - d, 1))

                start(factors_mate(p - d, x))

            @pl.when(p + d < nb)
            def _():
                for one in factors(p + d, 0):
                    one.wait_recv()

                @pl.when(p > 0)
                def _():
                    start(factors(p + d, 0))

                start(factors_mate(p + d, x))

    def starts_of():
        begin, found = jnp.int32(0), []
        for n in range(lengths.shape[1]):
            found.append(begin)
            begin = begin + lengths[0, n]
        return found

    def slots():
        token = lax.broadcasted_iota(jnp.int32, (1, TOK), 1)
        which = jnp.zeros((1, TOK), jnp.int32)
        for n, begin in enumerate(starts_of()):
            which = jnp.where(token >= begin, adapter_slot[request_adapter[0, n]], which)
        return which

    def low_copy(owner, m):
        return remote(lr.at[owner], lr.at[owner], lsend.at[m], lrecv.at[owner], row=(r + m) % nr)

    def lowrank_start():
        @pl.loop(0, nb)
        def _(b):
            factors_mate(b, other)[0].wait_recv()

        everything = lax.dot_general(
            dn[...].reshape(nc * 2 * rank, raw.shape[1]), raw[...],
            (((1,), (1,)), ((), ())), preferred_element_type=F32)
        which = slots()
        mine = jnp.zeros((2 * rank, TOK), F32)
        for a in range(nc):
            mine = mine + jnp.where(which == a, everything[a * 2 * rank:(a + 1) * 2 * rank], 0.0)
        lr[r] = mine

        @pl.loop(1, nr)
        def _(m):
            low_copy(r, m).start()

    def lowrank_end():
        @pl.loop(1, nr)
        def _(m):
            low_copy((r + m) % nr, m).wait_recv()

        @pl.loop(0, nb)
        def _(b):
            factors_mate(b, other)[1].wait_recv()

        total = lr[0]
        for o in range(1, nr):
            total = total + lr[o]
        which = slots()
        for ref, part in ((sq, total[:rank]), (sv, total[rank:])):
            tall = jnp.concatenate([jnp.where(which == a, part, 0.0) for a in range(nc)], axis=0)
            ref[...] = tall.T.astype(BF16)

    def tables():
        @pl.loop(0, TOK // TILE)
        def _(i):
            rows = pl.ds(pl.multiple_of(i * TILE, TILE), TILE)
            token = lax.broadcasted_iota(jnp.int32, (TILE, HEAD), 0) + i * TILE
            position = token
            for begin in starts_of():
                position = jnp.where(token >= begin, token - begin, position)
            angle = position.astype(F32) * freq[...]
            sign = jnp.where(lax.broadcasted_iota(jnp.int32, (TILE, HEAD), 1) < HEAD // 2, -1.0, 1.0)
            cosb[rows, :] = jnp.cos(angle)
            sinb[rows, :] = jnp.sin(angle) * sign

    def product(j, half, rows):
        total = None
        for o in range(nr):
            factor = wbuf[o * per:(o + 1) * per, j].reshape(per * kb, cw)
            term = jnp.dot(hid[o, half, rows, :], factor, preferred_element_type=F32)
            total = term if total is None else total + term
        return total

    def part_copy(j, h):
        rows = slice(h * HALF, (h + 1) * HALF)
        return remote(sendb.at[j, rows], precv.at[j, rows], psend.at[j, h], pget.at[j, h], col=mate)

    def compute(j):
        for h in range(2):
            @pl.loop(0, HALF // TILE)
            def _(i):
                rows = pl.ds(pl.multiple_of(h * HALF + i * TILE, TILE), TILE)
                sendb[j, rows, :] = product(j, other, rows).astype(BF16)

            part_copy(j, h).start()

        @pl.loop(0, TOK // TILE)
        def _(i):
            rows = pl.ds(pl.multiple_of(i * TILE, TILE), TILE)
            acc[j, rows, :] = product(j, x, rows)

    def combine(j):
        for h in range(2):
            part_copy(j, h).wait_recv()
            combine_half(j, h)

    def combine_half(j, h):
        @pl.loop(0, HALF // TILE)
        def _(i):
            rows = pl.ds(pl.multiple_of(h * HALF + i * TILE, TILE), TILE)
            v = acc[j, rows, :] + precv[j, rows, :].astype(F32)
            if j >= 2:
                at = (j - 2) * cw
                factor = up[:, :, at:at + cw].reshape(nc * rank, cw)
                lowered = sq if j < 6 else sv
                v = v + jnp.dot(lowered[rows, :], factor, preferred_element_type=F32)
            if j < 6:
                heads = []
                for k in range(cw // HEAD):
                    one = v[:, k * HEAD:(k + 1) * HEAD]
                    heads.append(one * cosb[rows, :] + pltpu.roll(one, HEAD // 2, 1) * sinb[rows, :])
                v = heads[0] if len(heads) == 1 else jnp.concatenate(heads, axis=1)
            v = v.astype(BF16)
            if j < 2:
                kv_out[rows, j * cw:(j + 1) * cw] = v
            elif j < 6:
                q_out[rows, (j - 2) * cw:(j - 1) * cw] = v
            else:
                kv_out[rows, kw + (j - 6) * cw:kw + (j - 5) * cw] = v

    to_mate().start()
    spread_hidden(x)
    send_own(0)
    send_factors()
    for j in range(1, AHEAD):
        send_own(j)
    tables()
    service(0)
    service_factors()
    from_mate().wait_recv()
    spread_hidden(other)
    pass_hidden(x)
    service(1)
    lowrank_start()
    service(2)
    pass_hidden(other)
    settle_hidden(x)
    settle_hidden(other)
    compute(0)
    service(3)
    compute(1)
    compute(2)
    lowrank_end()
    service(4)
    combine(0)
    compute(3)
    compute(4)
    combine(1)
    for j in range(5, CHUNKS):
        service(j)
        compute(j)
        combine(j - 3)
    for j in range(CHUNKS - 3, CHUNKS):
        combine(j)

    @pl.loop(0, CHUNKS)
    def _(j):
        @pl.loop(0, nb)
        def _(b):
            @pl.when((b <= p) & (p + 1 < nb))
            def _():
                weight(b, j, 1).wait_send()

            @pl.when((b >= p) & (p > 0))
            def _():
                weight(b, j, 0).wait_send()

    for j in range(CHUNKS):
        for h in range(2):
            part_copy(j, h).wait_send()

    @pl.loop(0, nb)
    def _(b):
        @pl.when((b <= p) & (p + 1 < nb))
        def _():
            for one in factors(b, 1):
                one.wait_send()

        @pl.when((b >= p) & (p > 0))
        def _():
            for one in factors(b, 0):
                one.wait_send()

        for one in factors_mate(b, x):
            one.wait_send()

    to_mate().wait_send()
    for t in range(2):
        for m in range(1, nr // 2):
            to_peer(t, m).wait_send()
        for m in range(nr // 2):
            to_twin((r + 2 * m) % nr, t).wait_send()

    @pl.loop(1, nr)
    def _(m):
        low_copy(r, m).wait_send()


def paging(lengths, table, kv, key, value):
    window = PAGE + 16
    kw = key.shape[2]
    row = lax.broadcasted_iota(jnp.int32, (PAGE, window), 0)
    column = lax.broadcasted_iota(jnp.int32, (PAGE, window), 1)
    spans, begin, begin_page = [], jnp.int32(0), jnp.int32(0)
    for n in range(lengths.shape[1]):
        length = lengths[0, n]
        spans.append((begin, begin_page, length))
        begin = begin + length
        begin_page = begin_page + (length + PAGE - 1) // PAGE
    for number in range(key.shape[0]):
        first, count = jnp.int32(0), jnp.int32(0)
        for begin, begin_page, length in spans:
            offset = (number - begin_page) * PAGE
            inside = (offset >= 0) & (offset < length)
            first = jnp.where(inside, begin + offset, first)
            count = jnp.where(inside, jnp.minimum(length - offset, PAGE), count)
        base = pl.multiple_of(jnp.minimum(first // 16 * 16, TOK - window), 16)
        pick = ((column == row + (first - base)) & (row < count)).astype(F32).astype(BF16)
        rows = jnp.dot(pick, kv[pl.ds(base, window), :], preferred_element_type=F32).astype(BF16)
        page = table[0, number]
        key[page] = rows[:, :kw]
        value[page] = rows[:, kw:]


def shards(nc, nr, hidden, w_query, w_key, w_value, adapter_down, adapter_up_query,
           adapter_up_value, lengths, request_adapter, adapter_slot, page_table):
    kb = w_query.shape[0]
    qw, kw = w_query.shape[1], w_key.shape[1]
    cw = (qw + 2 * kw) // CHUNKS
    hw = hidden.shape[1]
    rank = adapter_up_query.shape[1]
    pages = page_table.shape[1]
    nb = nc // 2

    frequency = np.exp(np.arange(HEAD // 2) * (-2.0 * math.log(10000.0) / HEAD))
    frequency = jnp.asarray(np.concatenate([frequency, frequency])[None, :], F32)
    down = adapter_down[0].T

    hbm = pl.BlockSpec(memory_space=pl.ANY)
    vmem = pl.BlockSpec(memory_space=pltpu.VMEM)
    smem = pl.BlockSpec(memory_space=pltpu.SMEM)
    dma = pltpu.SemaphoreType.DMA
    query, kv = pl.pallas_call(
        functools.partial(project, nc, nr),
        out_shape=(jax.ShapeDtypeStruct((TOK, qw), BF16), jax.ShapeDtypeStruct((TOK, 2 * kw), BF16)),
        in_specs=[vmem, hbm, hbm, hbm, hbm, hbm, hbm, vmem, smem, smem, smem],
        out_specs=(vmem, vmem),
        scratch_shapes=[
            pltpu.VMEM((nb, CHUNKS, kb, cw), BF16),
            pltpu.VMEM((2, TOK, hw // 2), BF16),
            pltpu.VMEM((nr, 2, TOK, hw // 2), BF16),
            pltpu.VMEM((CHUNKS, TOK, cw), F32),
            pltpu.VMEM((CHUNKS, TOK, cw), BF16),
            pltpu.VMEM((CHUNKS, TOK, cw), BF16),
            pltpu.VMEM((nc, 2 * rank, hw), BF16),
            pltpu.VMEM((nc, rank, qw + kw), BF16),
            pltpu.VMEM((nr, 2 * rank, TOK), F32),
            pltpu.VMEM((TOK, nc * rank), BF16),
            pltpu.VMEM((TOK, nc * rank), BF16),
            pltpu.VMEM((TOK, HEAD), F32),
            pltpu.VMEM((TOK, HEAD), F32),
            dma((CHUNKS,)),
            dma((3,)),
            dma((2, nb, CHUNKS)),
            dma((nb, CHUNKS)),
            dma((2, nr)),
            dma((nr, 2)),
            dma((nr, 2)),
            dma,
            dma,
            dma((CHUNKS, 2)),
            dma((CHUNKS, 2)),
            dma((2, nb)),
            dma((nb,)),
            dma((nc,)),
            dma((2, nb)),
            dma((nb,)),
            dma((nc,)),
            dma((nr,)),
            dma((nr,)),
        ],
        compiler_params=pltpu.CompilerParams(
            collective_id=0, has_side_effects=True, vmem_limit_bytes=60 * 1024 * 1024),
        name="project",
    )(hidden, w_query, w_key, w_value, down, adapter_up_query, adapter_up_value, frequency,
      lengths, request_adapter, adapter_slot)

    key_cache, value_cache = pl.pallas_call(
        paging,
        out_shape=(jax.ShapeDtypeStruct((pages, PAGE, kw), BF16),) * 2,
        in_specs=[smem, smem, vmem],
        out_specs=(vmem, vmem),
        compiler_params=pltpu.CompilerParams(vmem_limit_bytes=32 * 1024 * 1024),
        name="paging",
    )(lengths, page_table, kv)
    return (query, key_cache, value_cache)


def solution(mesh):
    return jax.shard_map(
        functools.partial(shards, mesh.shape["col"], mesh.shape["row"]),
        mesh=mesh,
        in_specs=(
            P("col", "row"),
            P("col", "row"),
            P("col", "row"),
            P("col", "row"),
            P("col", "row", None),
            P("col", None, "row"),
            P("col", None, "row"),
            P("col", None),
            P("col", None),
            P(),
            P("col", None),
        ),
        out_specs=(P("col", "row"), P("col", None, "row"), P("col", None, "row")),
        check_vma=False,
    )
```
